32 devices in a mesh: section: 2 (over x), ctx: 16 (over z, y, core).
Axes of the slice: x: 2, y: 2, z: 4, core: 2. Of those that a mesh axis runs over, the one named last changes fastest.
Arguments:
- doc_lengths: int32 [7], replicated, may hold values from 1 to 1152, 4096 in all
- queries: bfloat16 [4096, 8192], P('ctx', 'section'), may hold values from -6 to 6
- key_states: bfloat16 [4096, 1024], P('ctx', 'section'), may hold values from -6 to 6
- value_states: bfloat16 [4096, 1024], P('ctx', 'section'), may hold values from -6 to 6
Outputs:
- attended: bfloat16 [4096, 8192], P(('ctx', 'section'))
The draws below stay inside these ranges and needn't reach their ends.
Inputs may be any that keep to these rules, and one draw needn't show every extreme that they name: `doc_lengths`: they sum to 4096; the longest is exactly 1152.
All inputs are finite; a program needn't handle non-finite values.
Results may differ from the reference program's by a relative error of at most 0.0037.
Values may be sent and summed in bfloat16 or wider, within the bound.
A program may use at most 64 MiB of HBM per device.

```python
import math
import jax
import jax.numpy as jnp
import numpy as np
from jax import lax

Q_HEADS = 64
KV_HEADS = 8
HEAD = 128
TOK_DEV = 256
MOST = 1152
HOPS = 5
TOKENS = 4096
DOCS = 7


def base_field(key, width):
    return jnp.clip(jax.random.normal(key, (TOKENS, width), jnp.float32), -6.0, 6.0)


def draw_queries(key, part):
    sample_field = base_field(jax.random.fold_in(key, 1), Q_HEADS * HEAD)
    return sample_field.astype(jnp.bfloat16)


def draw_key_states(key, part):
    sample_field = base_field(jax.random.fold_in(key, 2), KV_HEADS * HEAD)
    return sample_field.astype(jnp.bfloat16)


def block_levels(stream_key, shape, pieces, low, high):
    def one(axis_at, shards_of):
        draws = jax.random.uniform(jax.random.fold_in(jax.random.fold_in(stream_key, 6), axis_at), (shards_of,), jnp.float32, low / len(pieces), high / len(pieces))
        return jnp.repeat(jnp.exp(draws), shape[axis_at] // shards_of).reshape((-1,) + (1,) * (len(shape) - axis_at - 1))

    level = one(*pieces[0])
    for cut in pieces[1:]:
        level = level * one(*cut)
    return level


def profile(count, total, most, slope):
    portions = [(1 << 20) // math.isqrt(grade ** slope) + 1 for grade in range(2, count + 1)]
    spare, holding = total - most - (count - 1), [1] * (count - 1)
    while spare > 0:
        free = [i for i in range(count - 1) if holding[i] < most]
        pool, budget = sum([portions[i] for i in free]), spare
        for i in free:
            more = min(most - holding[i], max(1, budget * portions[i] // pool), spare)
            holding[i] = holding[i] + more
            spare = spare - more
    return np.array([most] + holding)


def ragged(rng, amount, total, reach, skew):
    if amount == 2:
        one = jax.random.randint(rng, (), max(1, total - reach), min(reach, total - 1) + 1)
        return jnp.stack([one, total - one])
    lengths = jnp.asarray(profile(amount, total, reach, skew), jnp.int32)
    couples = (amount - 1) // 2
    donor, receiver = lengths[1:1 + 2 * couples:2], lengths[2:2 + 2 * couples:2]
    room = jnp.minimum(donor - 1, reach - receiver)
    passed = jax.random.randint(jax.random.fold_in(rng, 1), (couples,), 0, 1 << 20) % (room + 1)
    lengths = lengths.at[1:1 + 2 * couples:2].set(donor - passed).at[2:2 + 2 * couples:2].set(receiver + passed)
    return lengths[jax.random.permutation(jax.random.fold_in(rng, 2), amount)]


def centred(key, dims, deviation, most, shards=(), held_as=jnp.bfloat16):
    values = jax.random.normal(key, dims, jnp.float32) * deviation
    if len(shards) > 0:
        values = block_levels(key, dims, shards, -0.22, 0.18) * values
    return jnp.clip(values, min=-most, max=most).astype(held_as)


def setup_inputs(seed: int = 0) -> dict:
    arg_keys = jax.random.split(jax.random.key(seed), 5)
    doc_lengths = ragged(arg_keys[0], DOCS, TOKENS, MOST, 2).astype(jnp.int32)
    queries = draw_queries(jax.random.fold_in(arg_keys[4], 71), 0)
    key_states = draw_key_states(jax.random.fold_in(arg_keys[4], 71), 0)
    value_states = centred(arg_keys[3], (TOKENS, KV_HEADS * HEAD), 1.0, 6.0, ((0, 16), (1, 2)))
    return {"doc_lengths": doc_lengths, "queries": queries, "key_states": key_states, "value_states": value_states}


def document_of(doc_ends, positions):
    inside = lax.optimization_barrier(jnp.sum((doc_ends[None, :] <= positions[:, None]).astype(jnp.int32), axis=1))
    return jnp.where(positions < 0, -1, inside).astype(jnp.int32)

def reference(doc_lengths, queries, key_states, value_states):
    groups = Q_HEADS // KV_HEADS
    key_reach = HOPS * TOK_DEV
    width = key_reach + TOK_DEV
    doc_ends = jnp.cumsum(doc_lengths).astype(jnp.int32)
    padded_keys = jnp.concatenate([jnp.zeros((key_reach, KV_HEADS * HEAD), key_states.dtype), key_states], 0)
    padded_values = jnp.concatenate([jnp.zeros((key_reach, KV_HEADS * HEAD), value_states.dtype), value_states], 0)
    scale_factor = 1.0 / math.sqrt(HEAD)

    def one_block(block_index):
        start = (block_index * TOK_DEV).astype(jnp.int32)
        query_part = lax.dynamic_slice_in_dim(queries, start, TOK_DEV, 0).astype(jnp.float32)
        query_part = query_part.reshape(TOK_DEV, KV_HEADS, groups, HEAD)
        key_part = lax.dynamic_slice_in_dim(padded_keys, start, width, 0).astype(jnp.float32)
        key_part = key_part.reshape(width, KV_HEADS, HEAD)
        value_part = lax.dynamic_slice_in_dim(padded_values, start, width, 0).astype(jnp.float32)
        value_part = value_part.reshape(width, KV_HEADS, HEAD)
        query_pos = start + jnp.arange(TOK_DEV, dtype=jnp.int32)
        key_pos = start - key_reach + jnp.arange(width, dtype=jnp.int32)
        query_doc = document_of(doc_ends, query_pos)
        key_doc = document_of(doc_ends, key_pos)
        allowed = (query_doc[:, None] == key_doc[None, :]) & (key_pos[None, :] <= query_pos[:, None])
        scores = jnp.einsum('tkgd,skd->kgts', query_part, key_part) * scale_factor
        scores = jnp.where(allowed[None, None], scores, -jnp.inf)
        row_max = lax.optimization_barrier(jnp.max(scores, axis=3, keepdims=True))
        weights = jnp.exp(scores - row_max)
        row_sum = lax.optimization_barrier(jnp.sum(weights, axis=3))
        rounded = lax.optimization_barrier(weights.astype(jnp.bfloat16)).astype(jnp.float32)
        mixture = jnp.einsum('kgts,skd->tkgd', rounded, value_part)
        mixture = mixture / jnp.transpose(row_sum, (2, 0, 1))[:, :, :, None]
        return mixture.reshape(TOK_DEV, Q_HEADS * HEAD).astype(jnp.bfloat16)
    blocks = lax.map(one_block, jnp.arange(TOKENS // TOK_DEV, dtype=jnp.int32))
    return blocks.reshape(TOKENS, Q_HEADS * HEAD)
```

```python
import functools
import math

import jax
import jax.numpy as jnp
from jax import lax
from jax.experimental import pallas as pl
from jax.experimental.pallas import tpu as pltpu
from jax.sharding import PartitionSpec as P

Q_HEADS = 64
KV_HEADS = 8
HEAD = 128
MOST = 1152
GROUP = Q_HEADS // KV_HEADS
BLOCK = 128
MESH = pl.DeviceIdType.MESH
SCALE = math.log2(math.e) / math.sqrt(HEAD)
UP, SIDE, SIB_A, SIB_B, SIB_C, HALF_Y, HALF_Z = range(7)


def kernel(n_sec, n_ctx, docs_ref, q_ref, k_ref, v_ref, out_ref, kv, q, obuf, bias,
           in_sem, q_sem, send_sem, recv_sem, osend_sem, orecv_sem, own_sem):
    heads = kv.shape[0]
    tokens = q.shape[0]
    span = MOST + BLOCK
    rows_out = tokens // n_sec
    per_block = BLOCK // rows_out
    width = GROUP * HEAD
    sec = lax.axis_index("section")
    me = lax.axis_index("ctx")
    j = lax.rem(me, 2)
    pair = lax.div(me, 2)
    y = lax.rem(pair, 2)
    z = lax.div(pair, 2)
    n_z = n_ctx // 4
    low = 3 * 2 * tokens - MOST

    def rows(slot):
        return pl.ds(pl.multiple_of(slot * tokens - low, BLOCK), tokens)

    def half(start):
        return pl.ds(start, BLOCK)

    has_down = z > 0
    has_up = z < n_z - 1
    has_c = pair > 0
    is_giver = (y == 0) & (j == 1)

    half_y_src = half(3 * tokens - low + BLOCK)
    half_z_src = half(5 * tokens - low + BLOCK)

    def send(kind, h):
        src, dst, to = {
            UP: lambda: (rows(6 + j), rows(2 + j), me + 4),
            SIDE: lambda: (rows(6 + j - 4 * y), rows(4 + j), me + 2 - 4 * y),
            SIB_A: lambda: (rows(6), rows(6), me + 1),
            SIB_B: lambda: (rows(2 + j), rows(2 + j), me + 1 - 2 * j),
            SIB_C: lambda: (rows(4 + j), rows(4 + j), me + 1 - 2 * j),
            HALF_Y: lambda: (half_y_src, half(0), me + 1),
            HALF_Z: lambda: (half_z_src, half(0), me + 3),
        }[kind]()
        return pltpu.make_async_remote_copy(
            src_ref=kv.at[h, src], dst_ref=kv.at[h, dst],
            send_sem=send_sem.at[kind, h], recv_sem=recv_sem.at[kind, h],
            device_id={"ctx": to}, device_id_type=MESH)

    def wait_recv(kind, h):
        dst = {
            UP: lambda: rows(2 + j),
            SIDE: lambda: rows(4 + j),
            SIB_A: lambda: rows(6),
            SIB_B: lambda: rows(3 - j),
            SIB_C: lambda: rows(5 - j),
            HALF_Y: lambda: half(0),
            HALF_Z: lambda: half(0),
        }[kind]()
        pltpu.make_async_remote_copy(
            src_ref=kv.at[h, dst], dst_ref=kv.at[h, dst],
            send_sem=send_sem.at[kind, h], recv_sem=recv_sem.at[kind, h],
            device_id={"ctx": me}, device_id_type=MESH).wait_recv()

    def load(h, which):
        ref = (k_ref, v_ref)[which]
        return pltpu.make_async_copy(
            ref.at[:, pl.ds(h * HEAD, HEAD)],
            kv.at[h, rows(6 + j), pl.ds(which * HEAD, HEAD)], in_sem.at[which, h])

    def load_q():
        return pltpu.make_async_copy(q_ref, q, q_sem)

    for h in range(heads):
        load(h, 0).start()
        load(h, 1).start()
    load_q().start()

    barrier = pltpu.get_barrier_semaphore()
    greets = [(None, {"ctx": me + 1 - 2 * j}), (None, {"ctx": me + 2 - 4 * y}),
              (has_up, {"ctx": me + 4}), (has_down, {"ctx": me - 4}),
              (is_giver, {"ctx": me + 1}), ((y == 1) & (j == 0), {"ctx": me - 1}),
              (is_giver & has_up, {"ctx": me + 3}),
              ((y == 0) & (j == 0) & has_down, {"ctx": me - 3})]
    greets += [(None, {"section": lax.rem(sec + step, n_sec)}) for step in range(1, n_sec)]

    def when(condition, action):
        if condition is None:
            action()
        else:
            pl.when(condition)(action)

    for condition, to in greets:
        when(condition, functools.partial(
            pl.semaphore_signal, barrier, inc=1, device_id=to, device_id_type=MESH))
    peers = sum(1 if condition is None else jnp.where(condition, 1, 0)
                for condition, _ in greets)
    pl.semaphore_wait(barrier, peers)

    for h in range(heads):
        load(h, 0).wait()
        load(h, 1).wait()
        when(has_up, lambda: send(UP, h).start())
        when(y == 0, lambda: send(SIDE, h).start())
        when(j == 0, lambda: send(SIB_A, h).start())

    def clear(first, count):
        kv[:, first:first + count, :] = jnp.zeros((heads, count, 2 * HEAD), kv.dtype)

    when(z == 0, lambda: clear(2 * tokens - low, 2 * tokens))
    when(pair == 0, lambda: clear(4 * tokens - low, 2 * tokens))
    when((j == 0) & (pair < 3), lambda: clear(0, BLOCK))

    for b in range(tokens // BLOCK):
        first = me * tokens + b * BLOCK
        pos = first + lax.broadcasted_iota(jnp.int32, (BLOCK, 1), 0)
        start = jnp.zeros((BLOCK, 1), jnp.int32)
        end = jnp.int32(0)
        for d in range(docs_ref.shape[0]):
            end = end + docs_ref[d]
            start = jnp.where(pos >= end, end, start)
        key = first - MOST + lax.broadcasted_iota(jnp.int32, (BLOCK, span), 1)
        bias[b] = jnp.where((key >= start) & (key <= pos), 0.0, -1e30)

    def forward(h):
        @pl.when(has_down)
        def _():
            wait_recv(UP, h)
            when(y == 1, lambda: send(SIDE, h).start())
            send(SIB_B, h).start()
            when(is_giver, lambda: send(HALF_Y, h).start())

        @pl.when(has_c)
        def _():
            wait_recv(SIDE, h)
            send(SIB_C, h).start()
            when(is_giver & has_up, lambda: send(HALF_Z, h).start())

    def arrive(h):
        when(j == 1, lambda: wait_recv(SIB_A, h))
        when(has_down, lambda: wait_recv(SIB_B, h))
        when(has_c, lambda: wait_recv(SIB_C, h))
        when((y == 1) & (j == 0) & has_down, lambda: wait_recv(HALF_Y, h))
        when((y == 0) & (j == 0) & (z > 1), lambda: wait_recv(HALF_Z, h))

    def out_columns(source, h):
        return pl.ds(pl.multiple_of((source * heads + h) * width, width), width)

    def give(h, dest):
        piece = pl.ds(pl.multiple_of(dest * rows_out, rows_out), rows_out)
        return pltpu.make_async_remote_copy(
            src_ref=obuf.at[h, piece], dst_ref=out_ref.at[:, out_columns(sec, h)],
            send_sem=osend_sem.at[h, dest], recv_sem=orecv_sem.at[h, sec],
            device_id={"section": dest}, device_id_type=MESH)

    def take(h, source):
        piece = pl.ds(pl.multiple_of(source * rows_out, rows_out), rows_out)
        return pltpu.make_async_remote_copy(
            src_ref=obuf.at[h, piece], dst_ref=out_ref.at[:, out_columns(source, h)],
            send_sem=osend_sem.at[h, source], recv_sem=orecv_sem.at[h, source],
            device_id={"section": source}, device_id_type=MESH)

    def keep(h):
        piece = pl.ds(pl.multiple_of(sec * rows_out, rows_out), rows_out)
        return pltpu.make_async_copy(
            obuf.at[h, piece], out_ref.at[:, out_columns(sec, h)], own_sem.at[h])

    def unit(h, b):
        window = pl.ds(pl.multiple_of(j * tokens + b * BLOCK, BLOCK), span)
        lines = pl.ds(pl.multiple_of(b * BLOCK, BLOCK), BLOCK)
        keys = kv[h, window, 0:HEAD]
        values = jnp.concatenate(
            [kv[h, window, HEAD:2 * HEAD], jnp.ones((span, HEAD), kv.dtype)], 1)
        mask = bias[b]
        part = 4
        for first in range(0, GROUP, part):
            columns = pl.ds(pl.multiple_of(h * width + first * HEAD, HEAD), part * HEAD)
            wide = q[lines, columns]
            rows_q = jnp.concatenate(
                [wide[:, i * HEAD:(i + 1) * HEAD] for i in range(part)], 0)
            scores = lax.dot_general(rows_q, keys, (((1,), (1,)), ((), ())),
                                     preferred_element_type=jnp.float32)
            scores = (scores.reshape(part, BLOCK, span) + mask[None]).reshape(
                part * BLOCK, span)
            top = jnp.max(scores, axis=1, keepdims=True)
            weights = jnp.exp2((scores - top) * SCALE).astype(jnp.bfloat16)
            mixed = jnp.dot(weights, values, preferred_element_type=jnp.float32)
            result = (mixed[:, :HEAD] / mixed[:, HEAD:]).astype(obuf.dtype)
            for i in range(part):
                at = (first + i) * HEAD
                obuf[h, lines, at:at + HEAD] = result[i * BLOCK:(i + 1) * BLOCK]

    blocks = tokens // BLOCK
    my_block = lax.div(sec * rows_out, BLOCK)
    forward(0)
    load_q().wait()

    def step(t, carry):
        h = lax.div(t, blocks)
        turn = lax.rem(t, blocks)
        b = lax.rem(my_block + 1 + turn, blocks)

        when(turn == 0, lambda: arrive(h))
        when((turn == 1) & (h + 1 < heads), lambda: forward(h + 1))
        unit(h, b)
        for i in range(per_block):
            dest = b * per_block + i
            when(dest != sec, lambda: give(h, dest).start())
            when(dest == sec, lambda: keep(h).start())
        return carry

    lax.fori_loop(0, heads * blocks, step, 0)

    def finish(h, carry):
        when(has_up, lambda: send(UP, h).wait_send())
        when((y == 0) | has_down, lambda: send(SIDE, h).wait_send())
        when(j == 0, lambda: send(SIB_A, h).wait_send())
        when(has_down, lambda: send(SIB_B, h).wait_send())
        when(has_c, lambda: send(SIB_C, h).wait_send())
        when(is_giver & has_down, lambda: send(HALF_Y, h).wait_send())
        when(is_giver & has_down & has_up, lambda: send(HALF_Z, h).wait_send())
        keep(h).wait()
        for offset in range(1, n_sec):
            other = lax.rem(sec + offset, n_sec)
            give(h, other).wait_send()
            take(h, other).wait_recv()
        return carry

    lax.fori_loop(0, heads, finish, 0)


def per_device(n_sec, n_ctx, doc_lengths, queries, key_states, value_states):
    tokens = queries.shape[0]
    heads = key_states.shape[1] // HEAD
    span = MOST + BLOCK
    rows = 8 * tokens - (6 * tokens - MOST)
    dma = pltpu.SemaphoreType.DMA
    flops = 4 * tokens * span * heads * GROUP * HEAD
    return pl.pallas_call(
        functools.partial(kernel, n_sec, n_ctx),
        out_shape=jax.ShapeDtypeStruct((tokens // n_sec, Q_HEADS * HEAD), jnp.bfloat16),
        in_specs=[pl.BlockSpec(memory_space=pltpu.SMEM)]
        + [pl.BlockSpec(memory_space=pl.ANY)] * 3,
        out_specs=pl.BlockSpec(memory_space=pl.ANY),
        scratch_shapes=[
            pltpu.VMEM((heads, rows, 2 * HEAD), jnp.bfloat16),
            pltpu.VMEM(queries.shape, jnp.bfloat16),
            pltpu.VMEM((heads, tokens, GROUP * HEAD), jnp.bfloat16),
            pltpu.VMEM((tokens // BLOCK, BLOCK, span), jnp.float32),
            dma((2, heads)),
            dma,
            dma((7, heads)),
            dma((7, heads)),
            dma((heads, n_sec)),
            dma((heads, n_sec)),
            dma((heads,)),
        ],
        compiler_params=pltpu.CompilerParams(
            collective_id=0, has_side_effects=True, vmem_limit_bytes=48 * 1024 * 1024),
        cost_estimate=pl.CostEstimate(
            flops=flops, bytes_accessed=5 * 1024 * 1024,
            transcendentals=tokens * span * heads * GROUP),
    )(doc_lengths, queries, key_states, value_states)


def solution(mesh):
    return jax.shard_map(
        functools.partial(per_device, mesh.shape["section"], mesh.shape["ctx"]),
        mesh=mesh,
        in_specs=(P(), P("ctx", "section"), P("ctx", "section"), P("ctx", "section")),
        out_specs=P(("ctx", "section"), None),
        check_vma=False,
    )
```

```python
import functools
import math

import jax
import jax.numpy as jnp
from jax import lax
from jax.experimental import pallas as pl
from jax.experimental.pallas import tpu as pltpu
from jax.sharding import PartitionSpec as P

Q_HEADS = 64
KV_HEADS = 8
HEAD = 128
MOST = 1152
GROUP = Q_HEADS // KV_HEADS
BLOCK = 128
MESH = pl.DeviceIdType.MESH
RELAY_AFTER = {(0, 1, 1): 2, (0, 2, 0): 1, (0, 2, 1): 1, (1, 1, 1): 2, (1, 2, 1): 1, (2, 1, 1): 1}
SCALE = math.log2(math.e) / math.sqrt(HEAD)
HALVES = 2
PART = GROUP // HALVES
UP, SIDE, SIB_A, SIB_B, SIB_C, HALF_Y, HALF_Z = range(7)


def kernel(n_sec, n_ctx, docs_ref, q_ref, k_ref, v_ref, out_ref, kv, q, qx, obuf, bias,
           in_sem, q_sem, send_sem, recv_sem, osend_sem, orecv_sem, own_sem, x_send, x_recv):
    heads = k_ref.shape[1] // HEAD
    extra = kv.shape[0] - heads
    kvs = kv.shape[0]
    tokens = q.shape[0]
    span = MOST + BLOCK
    rows_out = tokens // n_sec
    per_block = BLOCK // rows_out
    width = GROUP * HEAD
    sec = lax.axis_index("section")
    me = lax.axis_index("ctx")
    j = lax.rem(me, 2)
    pair = lax.div(me, 2)
    y = lax.rem(pair, 2)
    z = lax.div(pair, 2)
    n_z = n_ctx // 4
    low = 3 * 2 * tokens - MOST

    def rows(slot):
        return pl.ds(pl.multiple_of(slot * tokens - low, BLOCK), tokens)

    def half(start):
        return pl.ds(start, BLOCK)

    has_down = z > 0
    has_up = z < n_z - 1
    has_c = pair > 0
    is_giver = (y == 0) & (j == 1)

    half_y_src = half(3 * tokens - low + BLOCK)
    half_z_src = half(5 * tokens - low + BLOCK)

    def send(kind, h):
        src, dst, to = {
            UP: lambda: (rows(6 + j), rows(2 + j), me + 4),
            SIDE: lambda: (rows(6 + j - 4 * y), rows(4 + j), me + 2 - 4 * y),
            SIB_A: lambda: (rows(6), rows(6), me + 1),
            SIB_B: lambda: (rows(2 + j), rows(2 + j), me + 1 - 2 * j),
            SIB_C: lambda: (rows(4 + j), rows(4 + j), me + 1 - 2 * j),
            HALF_Y: lambda: (half_y_src, half(0), me + 1),
            HALF_Z: lambda: (half_z_src, half(0), me + 3),
        }[kind]()
        return pltpu.make_async_remote_copy(
            src_ref=kv.at[h, src], dst_ref=kv.at[h, dst],
            send_sem=send_sem.at[kind, h], recv_sem=recv_sem.at[kind, h],
            device_id={"ctx": to}, device_id_type=MESH)

    def wait_recv(kind, h):
        dst = {
            UP: lambda: rows(2 + j),
            SIDE: lambda: rows(4 + j),
            SIB_A: lambda: rows(6),
            SIB_B: lambda: rows(3 - j),
            SIB_C: lambda: rows(5 - j),
            HALF_Y: lambda: half(0),
            HALF_Z: lambda: half(0),
        }[kind]()
        pltpu.make_async_remote_copy(
            src_ref=kv.at[h, dst], dst_ref=kv.at[h, dst],
            send_sem=send_sem.at[kind, h], recv_sem=recv_sem.at[kind, h],
            device_id={"ctx": me}, device_id_type=MESH).wait_recv()

    def load(h, which):
        ref = (k_ref, v_ref)[which]
        return pltpu.make_async_copy(
            ref.at[:, pl.ds(h * HEAD, HEAD)],
            kv.at[h, rows(6 + j), pl.ds(which * HEAD, HEAD)], in_sem.at[which, h])

    def load_q():
        return pltpu.make_async_copy(q_ref, q, q_sem)

    for h in range(heads):
        load(h, 0).start()
        load(h, 1).start()
    load_q().start()

    barrier = pltpu.get_barrier_semaphore()
    greets = [(None, {"ctx": me + 1 - 2 * j}), (None, {"ctx": me + 2 - 4 * y}),
              (has_up, {"ctx": me + 4}), (has_down, {"ctx": me - 4}),
              (is_giver, {"ctx": me + 1}), ((y == 1) & (j == 0), {"ctx": me - 1}),
              (is_giver & has_up, {"ctx": me + 3}),
              ((y == 0) & (j == 0) & has_down, {"ctx": me - 3})]
    greets += [(None, {"section": lax.rem(sec + step, n_sec)}) for step in range(1, n_sec)]

    def when(condition, action):
        if condition is None:
            action()
        else:
            pl.when(condition)(action)

    for condition, to in greets:
        when(condition, functools.partial(
            pl.semaphore_signal, barrier, inc=1, device_id=to, device_id_type=MESH))
    peers = sum(1 if condition is None else jnp.where(condition, 1, 0)
                for condition, _ in greets)
    pl.semaphore_wait(barrier, peers)

    def spread(h):
        when(has_up, lambda: send(UP, h).start())
        when(y == 0, lambda: send(SIDE, h).start())
        when(j == 0, lambda: send(SIB_A, h).start())

    def cross_kv():
        return pltpu.make_async_remote_copy(
            src_ref=kv.at[heads - 1, rows(6 + j)], dst_ref=kv.at[heads, rows(6 + j)],
            send_sem=x_send.at[0], recv_sem=x_recv.at[0],
            device_id={"section": 1 - sec}, device_id_type=MESH)

    def cross_q():
        theirs = pl.ds(pl.multiple_of((1 - sec) * BLOCK, BLOCK), BLOCK)
        return pltpu.make_async_remote_copy(
            src_ref=q_ref.at[theirs, pl.ds((heads - 1) * width, width)], dst_ref=qx,
            send_sem=x_send.at[1], recv_sem=x_recv.at[1],
            device_id={"section": 1 - sec}, device_id_type=MESH)

    for h in [heads - 1] * extra + list(range(heads - extra)):
        load(h, 0).wait()
        load(h, 1).wait()
        if extra and h == heads - 1:
            cross_kv().start()
            cross_q().start()
        else:
            spread(h)
    if extra:
        spread(heads - 1)

    def clear(first, count):
        kv[:, first:first + count, :] = jnp.zeros((kvs, count, 2 * HEAD), kv.dtype)

    when(z == 0, lambda: clear(2 * tokens - low, 2 * tokens))
    when(pair == 0, lambda: clear(4 * tokens - low, 2 * tokens))
    when((j == 0) & (pair < 3), lambda: clear(0, BLOCK))

    for b in range(tokens // BLOCK):
        first = me * tokens + b * BLOCK
        pos = first + lax.broadcasted_iota(jnp.int32, (BLOCK, 1), 0)
        start = jnp.zeros((BLOCK, 1), jnp.int32)
        end = jnp.int32(0)
        for d in range(docs_ref.shape[0]):
            end = end + docs_ref[d]
            start = jnp.where(pos >= end, end, start)
        key = first - MOST + lax.broadcasted_iota(jnp.int32, (BLOCK, span), 1)
        bias[b] = jnp.where((key >= start) & (key <= pos), 0.0, -1e30)

    def forward_up(h):
        @pl.when(has_down)
        def _():
            wait_recv(UP, h)
            when(y == 1, lambda: send(SIDE, h).start())
            send(SIB_B, h).start()
            when(is_giver, lambda: send(HALF_Y, h).start())

    def forward_side(h):
        @pl.when(has_c)
        def _():
            wait_recv(SIDE, h)
            send(SIB_C, h).start()
            when(is_giver & has_up, lambda: send(HALF_Z, h).start())

    def spread_cross():
        cross_kv().wait_recv()
        spread(heads)

    def arrive(h):
        when(j == 1, lambda: wait_recv(SIB_A, h))
        when(has_down, lambda: wait_recv(SIB_B, h))
        when(has_c, lambda: wait_recv(SIB_C, h))
        when((y == 1) & (j == 0) & has_down, lambda: wait_recv(HALF_Y, h))
        when((y == 0) & (j == 0) & (z > 1), lambda: wait_recv(HALF_Z, h))

    def out_columns(source, h, p):
        first = (source * heads + h) * width + p * PART * HEAD
        return pl.ds(pl.multiple_of(first, PART * HEAD), PART * HEAD)

    def columns(p):
        return pl.ds(p * PART * HEAD, PART * HEAD)

    def piece(dest):
        return pl.ds(pl.multiple_of(dest * rows_out, rows_out), rows_out)

    def give(h, p, dest):
        return pltpu.make_async_remote_copy(
            src_ref=obuf.at[h, piece(dest), columns(p)],
            dst_ref=out_ref.at[:, out_columns(sec, h, p)],
            send_sem=osend_sem.at[h, p, dest], recv_sem=orecv_sem.at[h, p, sec],
            device_id={"section": dest}, device_id_type=MESH)

    def take(h, p, source):
        return pltpu.make_async_remote_copy(
            src_ref=obuf.at[h, piece(source), columns(p)],
            dst_ref=out_ref.at[:, out_columns(source, h, p)],
            send_sem=osend_sem.at[h, p, source], recv_sem=orecv_sem.at[h, p, source],
            device_id={"section": source}, device_id_type=MESH)

    def keep(h, p):
        at = out_columns(sec, h, p) if h < heads else out_columns(1 - sec, heads - 1, p)
        return pltpu.make_async_copy(
            obuf.at[h, piece(sec), columns(p)], out_ref.at[:, at], own_sem.at[h, p])

    def work(h, b, p):
        window = pl.ds(pl.multiple_of(j * tokens + b * BLOCK, BLOCK), span)
        lines = pl.ds(pl.multiple_of(b * BLOCK, BLOCK), BLOCK)
        keys = kv[h, window, 0:HEAD]
        values = jnp.concatenate(
            [kv[h, window, HEAD:2 * HEAD], jnp.ones((span, HEAD), kv.dtype)], 1)
        mask = bias[b]
        if h < heads:
            wide = q[lines, h * width + p * PART * HEAD:h * width + (p + 1) * PART * HEAD]
        else:
            wide = qx[:, p * PART * HEAD:(p + 1) * PART * HEAD]
        rows_q = jnp.concatenate([wide[:, i * HEAD:(i + 1) * HEAD] for i in range(PART)], 0)
        scores = lax.dot_general(rows_q, keys, (((1,), (1,)), ((), ())),
                                 preferred_element_type=jnp.float32)
        scores = (scores.reshape(PART, BLOCK, span) + mask[None]).reshape(PART * BLOCK, span)
        top = jnp.max(scores, axis=1, keepdims=True)
        weights = jnp.exp2((scores - top) * SCALE).astype(jnp.bfloat16)
        mixed = jnp.dot(weights, values, preferred_element_type=jnp.float32)
        result = (mixed[:, :HEAD] / mixed[:, HEAD:]).astype(obuf.dtype)
        for i in range(PART):
            at = (p * PART + i) * HEAD
            obuf[h, lines, at:at + HEAD] = result[i * BLOCK:(i + 1) * BLOCK]

    def half_unit(h, b, p):
        work(h, b, p)
        for i in range(per_block):
            dest = b * per_block + i
            when(dest != sec, lambda: give(h, p, dest).start())
            when(dest == sec, lambda: keep(h, p).start())

    blocks = tokens // BLOCK
    my_block = lax.div(sec * rows_out, BLOCK)
    units = [(h, turn) for h in range(heads - extra) for turn in range(1, blocks + 1)]
    units += [(h, blocks) for h in range(heads - extra, kvs)]

    relays = [functools.partial(forward_up, 0)]
    if extra:
        relays.append(spread_cross)
    for h in range(kvs):
        if h + 1 < kvs:
            relays.append(functools.partial(forward_up, h + 1))
        relays.append(functools.partial(forward_side, h))
    due = {}
    for h in range(kvs):
        due[h] = 1 + extra + 2 * (h + 1) - (h + 1 == kvs)

    done = 0
    reached = -1
    load_q_waited = False
    for h, turn in units:
        if h > reached:
            while done < due[h]:
                relays[done]()
                done += 1
            if not load_q_waited:
                load_q().wait()
                load_q_waited = True
            arrive(h)
            if h == heads:
                cross_q().wait_recv()
            reached = h
        b = lax.rem(my_block + turn, blocks)
        for p in range(HALVES):
            half_unit(h, b, p)
            if done < len(relays) and (h, turn, p) in RELAY_AFTER:
                for _ in range(RELAY_AFTER[h, turn, p]):
                    relays[done]()
                    done += 1

    for h in range(kvs):
        when(has_up, lambda: send(UP, h).wait_send())
        when((y == 0) | has_down, lambda: send(SIDE, h).wait_send())
        when(j == 0, lambda: send(SIB_A, h).wait_send())
        when(has_down, lambda: send(SIB_B, h).wait_send())
        when(has_c, lambda: send(SIB_C, h).wait_send())
        when(is_giver & has_down, lambda: send(HALF_Y, h).wait_send())
        when(is_giver & has_down & has_up, lambda: send(HALF_Z, h).wait_send())
        for p in range(HALVES):
            keep(h, p).wait()
    if extra:
        cross_kv().wait_send()
        cross_q().wait_send()
    for h in range(heads - extra):
        for p in range(HALVES):
            for offset in range(1, n_sec):
                other = lax.rem(sec + offset, n_sec)
                give(h, p, other).wait_send()
                take(h, p, other).wait_recv()


def per_device(n_sec, n_ctx, doc_lengths, queries, key_states, value_states):
    tokens = queries.shape[0]
    heads = key_states.shape[1] // HEAD
    span = MOST + BLOCK
    extra = int(n_sec == 2 and heads > 1)
    kvs = heads + extra
    rows = 8 * tokens - (6 * tokens - MOST)
    dma = pltpu.SemaphoreType.DMA
    flops = 4 * tokens * span * heads * GROUP * HEAD
    return pl.pallas_call(
        functools.partial(kernel, n_sec, n_ctx),
        out_shape=jax.ShapeDtypeStruct((tokens // n_sec, Q_HEADS * HEAD), jnp.bfloat16),
        in_specs=[pl.BlockSpec(memory_space=pltpu.SMEM)]
        + [pl.BlockSpec(memory_space=pltpu.HBM)] * 3,
        out_specs=pl.BlockSpec(memory_space=pl.ANY),
        scratch_shapes=[
            pltpu.VMEM((kvs, rows, 2 * HEAD), jnp.bfloat16),
            pltpu.VMEM(queries.shape, jnp.bfloat16),
            pltpu.VMEM((BLOCK, GROUP * HEAD), jnp.bfloat16),
            pltpu.VMEM((kvs, tokens, GROUP * HEAD), jnp.bfloat16),
            pltpu.VMEM((tokens // BLOCK, BLOCK, span), jnp.float32),
            dma((2, heads)),
            dma,
            dma((7, kvs)),
            dma((7, kvs)),
            dma((heads, HALVES, n_sec)),
            dma((heads, HALVES, n_sec)),
            dma((kvs, HALVES)),
            dma((2,)),
            dma((2,)),
        ],
        compiler_params=pltpu.CompilerParams(
            collective_id=0, has_side_effects=True, vmem_limit_bytes=60 * 1024 * 1024),
        cost_estimate=pl.CostEstimate(
            flops=flops, bytes_accessed=5 * 1024 * 1024,
            transcendentals=tokens * span * heads * GROUP),
    )(doc_lengths, queries, key_states, value_states)


def solution(mesh):
    return jax.shard_map(
        functools.partial(per_device, mesh.shape["section"], mesh.shape["ctx"]),
        mesh=mesh,
        in_specs=(P(), P("ctx", "section"), P("ctx", "section"), P("ctx", "section")),
        out_specs=P(("ctx", "section"), None),
        check_vma=False,
    )
```
